768 devices in a mesh: dp: 12 (over z), block: 64 (over y, x, core).
Axes of the slice: x: 4, y: 8, z: 12, core: 2. Of those that a mesh axis runs over, the one named last changes fastest.
Arguments:
- grad_part: bfloat16 [12, 192, 512, 512], P('dp', None, 'block'), may hold values from -1.796875 to 1.796875
- owner_table: int32 [192], P('dp'), may hold values from 0 to 63, as said below
- left_stats: bfloat16 [12, 64, 512, 512], P('dp', 'block'), may hold values from -16 to 16384, as said below
- right_stats: bfloat16 [12, 64, 512, 512], P('dp', 'block'), may hold values from -16 to 16384, as said below
Outputs:
- update: bfloat16 [192, 512, 512], P('dp', 'block')
The draws below stay inside these ranges and needn't reach their ends.
Inputs may be any that keep to these rules, and one draw needn't show every extreme that they name: `owner_table`: within each group of 16 consecutive entries no owner is named twice. `left_stats`: every 512 x 512 matrix is symmetric and positive definite. `right_stats`: every 512 x 512 matrix is symmetric and positive definite.
All inputs are finite; a program needn't handle non-finite values. Where the reference program divides by a largest or mean magnitude, that divisor is 1e-20 or more.
Results may differ from the reference program's by a relative error of at most 0.023.
Values may be sent and summed in bfloat16 or wider, within the bound.
A program may use at most 32 MiB of HBM per device.

```python
import jax
import jax.numpy as jnp
from jax import lax

B = 512
NB_GRP = 16
NBLK = 192
N_DP = 12
N_BLOCK = 64


def stat_matrices(key):
    first_key, second_key = jax.random.split(key, 2)
    shape = (N_DP, N_BLOCK, B, B)
    uniform_part = jax.random.uniform(first_key, shape, jnp.float32, -1.0, 1.0)
    symmetric = 0.5 * (uniform_part + jnp.swapaxes(uniform_part, -1, -2))
    diagonal = B * (1.0 + jax.random.uniform(second_key, shape[:-1], jnp.float32))
    identity = jnp.eye(B, dtype=jnp.float32)
    matrix = symmetric * (1.0 - identity) + identity * diagonal[..., :, None]
    return matrix.astype(jnp.bfloat16)


def draw_left_stats(key, part):
    key = jax.random.fold_in(key, 21)
    return stat_matrices(key)


def draw_right_stats(key, part):
    key = jax.random.fold_in(key, 37)
    return stat_matrices(key)


def draw_owner_table(key, part):
    key = jax.random.fold_in(key, 53)
    group_keys = jax.random.split(key, N_DP)

    def one_group(group_key):
        return jax.random.permutation(group_key, N_BLOCK)[:NB_GRP]
    return jax.vmap(one_group)(group_keys).reshape(-1).astype(jnp.int32)


def with_spikes(drawn, rng, source, target, parts, factor):
    def block_of(axis_at):
        return (jnp.arange(drawn.shape[axis_at]) // (drawn.shape[axis_at] // parts)).reshape((-1,) + (1,) * (drawn.ndim - 1 - axis_at))

    near = jax.random.permutation(rng, parts)[block_of(target)]
    other_side = (block_of(target) + parts // 2) % parts
    return jnp.where((block_of(source) == near) | (block_of(source) == other_side), factor * drawn, drawn)


def block_levels(rng, dims, pieces, smallest, largest):
    def one(dim, blocks):
        steps = jax.random.uniform(jax.random.fold_in(jax.random.fold_in(rng, 6), dim), (blocks,), jnp.float32, smallest / len(pieces), largest / len(pieces))
        return jnp.repeat(jnp.exp(steps), dims[dim] // blocks).reshape((-1,) + (1,) * (len(dims) - dim - 1))

    level = one(*pieces[0])
    for cut in pieces[1:]:
        level = level * one(*cut)
    return level


def noise_with(rng, dims, scale, most, pieces, heavy, kind=jnp.bfloat16):
    result = scale * jax.random.normal(rng, dims, jnp.float32)
    if pieces:
        result = result * block_levels(rng, dims, pieces, -0.22, 0.18)
    return jnp.clip(with_spikes(result, jax.random.fold_in(rng, 3), *heavy), -most, most).astype(kind)


def setup_inputs(seed: int = 0) -> dict:
    arg_keys = jax.random.split(jax.random.key(seed), 5)
    grad_part = noise_with(arg_keys[0], (N_DP, NBLK, B, B), 0.3, 1.796875, ((0, 12), (2, 64)), (0, 1, 12, 2.0))
    owner_table = draw_owner_table(jax.random.fold_in(arg_keys[4], 71), 0)
    left_stats = draw_left_stats(jax.random.fold_in(arg_keys[4], 71), 0)
    right_stats = draw_right_stats(jax.random.fold_in(arg_keys[4], 71), 0)
    return {"grad_part": grad_part, "owner_table": owner_table, "left_stats": left_stats, "right_stats": right_stats}


DECAY = 0.9
EPSILON = 1e-06

def batched(pattern, left_side, right_side):
    return jnp.einsum(pattern, left_side.astype(jnp.float32), right_side.astype(jnp.float32))

def inverse_root(statistic):
    row_bound = lax.optimization_barrier(jnp.max(lax.optimization_barrier(jnp.sum(jnp.abs(statistic), axis=-1)), axis=-1))[..., None, None]
    scaled = statistic / row_bound
    scaled_low = scaled.astype(jnp.bfloat16)
    square = batched('sij,sjk->sik', scaled_low, scaled_low)
    square_low = lax.optimization_barrier(square.astype(jnp.bfloat16))
    mixed_low = (square_low.astype(jnp.float32) - 9.0 * scaled).astype(jnp.bfloat16)
    quartic = batched('sij,sjk->sik', square_low, mixed_low)
    identity = jnp.eye(statistic.shape[-1], dtype=jnp.float32)
    root_value = 36.0 * identity - 39.0 * scaled + 27.0 * square_low.astype(jnp.float32) + quartic
    return root_value.astype(jnp.bfloat16)

def precondition(grad_block, left_prev, right_prev):
    left_stat = DECAY * left_prev.astype(jnp.float32) + (1.0 - DECAY) * batched('sij,skj->sik', grad_block, grad_block)
    right_stat = DECAY * right_prev.astype(jnp.float32) + (1.0 - DECAY) * batched('sji,sjk->sik', grad_block, grad_block)
    left_root = inverse_root(left_stat)
    right_root = inverse_root(right_stat)
    half_done = batched('sij,sjk->sik', left_root, grad_block).astype(jnp.bfloat16)
    precond = batched('sij,sjk->sik', half_done, right_root)
    grad_wide = grad_block.astype(jnp.float32)
    grad_power = lax.optimization_barrier(jnp.mean(grad_wide * grad_wide, axis=(1, 2), keepdims=True))
    cond_power = lax.optimization_barrier(jnp.mean(precond * precond, axis=(1, 2), keepdims=True))
    graft_scale = jnp.sqrt(grad_power) / jnp.sqrt(cond_power + EPSILON)
    return (precond * graft_scale).astype(jnp.bfloat16)

def reference(grad_part, owner_table, left_stats, right_stats):

    def one_block(number):
        group_index = (number // NB_GRP).astype(jnp.int32)
        owner_index = owner_table[number]
        summed = lax.optimization_barrier(jnp.sum(grad_part[:, number].astype(jnp.float32), axis=0))
        grad_block = summed.astype(jnp.bfloat16)[None]
        left_prev = left_stats[group_index, owner_index][None]
        right_prev = right_stats[group_index, owner_index][None]
        return precondition(grad_block, left_prev, right_prev)[0]
    return lax.map(one_block, jnp.arange(NBLK, dtype=jnp.int32))
```

```python
import functools

import jax
import jax.numpy as jnp
from jax import lax
from jax.experimental import pallas as pl
from jax.experimental.pallas import tpu as pltpu
from jax.sharding import PartitionSpec as P

DECAY = 0.9
EPSILON = 1e-06
MESH = pl.DeviceIdType.MESH
F32 = jnp.float32
BF16 = jnp.bfloat16


def site_of(j):
    return 4 * j + 2 * lax.rem(j // 2, 2)


def wide_dot(a, b, contract):
    return lax.dot_general(a, b, ((contract[0], contract[1]), ((), ())), preferred_element_type=F32)


def kernel(nz, nb, grp, table, gp, left, right, out,
           zrecv, zstage, gbuf, statbuf, selbuf, statfull, g_ref, gt_ref,
           wide_l, wide_r, low_l, low_r, sq_l, sq_r, mix_l, mix_r, upd, rbuf,
           z_send, z_recv, g_send, g_recv, s_send, s_recv, f_send, f_recv, u_send, u_recv, local_sem):
    z = lax.axis_index("dp")
    me = lax.axis_index("block")
    order = 8 * nb
    cw = order // 4
    rows = grp * 8
    half = nz // 2
    own_site = me // 4
    is_site = me == site_of(own_site)

    def there(dp, block):
        return {"dp": dp, "block": block}

    barrier = pltpu.get_barrier_semaphore()
    up, down = lax.rem(z + 1, nz), lax.rem(z + nz - 1, nz)
    for neighbour in (up, down):
        pl.semaphore_signal(barrier, inc=1, device_id=there(neighbour, me), device_id_type=MESH)

    @pl.loop(1, nb)
    def _(r):
        pl.semaphore_signal(barrier, inc=1, device_id=there(z, lax.rem(me + r, nb)), device_id_type=MESH)

    pl.semaphore_wait(barrier, nb + 1)

    def column(k):
        return pl.ds(k * cw, cw)

    def own_rows(d):
        return pl.ds(pl.multiple_of(d * rows, rows), rows)

    def arc(k, way):
        return half if (k + way) % 2 == 0 else half - 1

    def hop(src, way, k, s):
        return pltpu.make_async_remote_copy(
            src_ref=src, dst_ref=zrecv.at[way, k, s],
            send_sem=z_send.at[way, k, s], recv_sem=z_recv.at[way, k, s],
            device_id=there(up if way == 0 else down, me), device_id_type=MESH)

    def target(way, dist):
        return lax.rem(z + dist, nz) if way == 0 else lax.rem(z + nz - dist, nz)

    def begin(s):
        for k in range(4):
            for way in range(2):
                if half - arc(k, way) == s:
                    d = target(way, half - s)
                    hop(gp.at[own_rows(d), column(k)], way, k, s).start()

    def onward(s, k, way):
        held = zrecv.at[way, k, s - 1]
        hop(held, way, k, s - 1).wait_recv()
        d = target(way, half - s)
        held[...] = (held[...].astype(F32) + gp[own_rows(d), column(k)].astype(F32)).astype(BF16)
        hop(held, way, k, s).start()

    begin(0)
    begin(1)

    def stat_copy(source, first, d, who):
        return pltpu.make_async_remote_copy(
            src_ref=source.at[pl.ds(pl.multiple_of(first, 16), 16)], dst_ref=statbuf.at[me],
            send_sem=s_send, recv_sem=s_recv, device_id=there(z, who), device_id_type=MESH)

    hb = nb // 2

    @pl.loop(1, nb)
    def _(r):
        d = lax.rem(me + r, nb)

        @pl.when(d < hb)
        def _():
            stat_copy(left, 16 * d, d, d).start()

        @pl.when(d >= hb)
        def _():
            stat_copy(right, 16 * (d - hb), d, d).start()

    @pl.when(me < hb)
    def _():
        c = pltpu.make_async_copy(left.at[pl.ds(pl.multiple_of(16 * me, 16), 16)], statbuf.at[me], local_sem)
        c.start()
        c.wait()

    @pl.when(me >= hb)
    def _():
        c = pltpu.make_async_copy(right.at[pl.ds(pl.multiple_of(16 * (me - hb), 16), 16)], statbuf.at[me], local_sem)
        c.start()
        c.wait()

    for k in range(4):
        for way in range(2):
            if arc(k, way) == half:
                onward(1, k, way)

    @pl.loop(2, half)
    def _(s):
        for k in range(4):
            for way in range(2):
                onward(s, k, way)

    for w in range(2):
        parts = []
        for k in (2 * w, 2 * w + 1):
            for way in range(2):
                hop(zrecv.at[way, k, half - 1], way, k, half - 1).wait_recv()
            total = (gp[own_rows(z), column(k)].astype(F32) + zrecv[0, k, half - 1].astype(F32)
                     + zrecv[1, k, half - 1].astype(F32))
            parts.append(total.reshape(grp, 8, cw))
        zstage[w] = jnp.concatenate(parts, axis=1).astype(BF16)

        @pl.loop(0, grp)
        def _(i):
            j = lax.rem(own_site + i, grp)
            who = site_of(j)

            @pl.when(who != me)
            def _():
                pltpu.make_async_remote_copy(
                    src_ref=zstage.at[w, j], dst_ref=gbuf.at[w, me],
                    send_sem=g_send.at[w], recv_sem=g_recv.at[w],
                    device_id=there(z, who), device_id_type=MESH).start()

        @pl.when(is_site)
        def _():
            gbuf[w, me] = zstage[w, own_site]

    def settle(ref, sem):
        pltpu.make_async_copy(ref, ref, sem).wait()

    settle(statbuf.at[pl.ds(0, nb - 1)], s_recv)

    @pl.loop(0, grp)
    def _(i):
        j = lax.rem(own_site + i, grp)
        selbuf[j] = statbuf[table[j]]
        who = site_of(j)

        @pl.when(who != me)
        def _():
            pltpu.make_async_remote_copy(
                src_ref=selbuf.at[j], dst_ref=statfull.at[me],
                send_sem=f_send, recv_sem=f_recv,
                device_id=there(z, who), device_id_type=MESH).start()

    @pl.when(is_site)
    def _():
        statfull[me] = selbuf[own_site]

    @pl.when(is_site)
    def _():
        for w in range(2):
            settle(gbuf.at[w, pl.ds(0, nb - 1)], g_recv.at[w])
            pieces = gbuf[w].astype(F32).reshape(nb, 2, 8, cw)
            for h in range(2):
                piece = pieces[:, h].reshape(order, cw).astype(BF16)
                g_ref[:, column(2 * w + h)] = piece
                gt_ref[column(2 * w + h), :] = piece.T
        settle(statfull.at[pl.ds(0, nb - 1)], f_recv)
        nr = 2
        rb = order // nr
        blocks = [pl.ds(i * rb, rb) for i in range(nr)]
        sides = ((0, g_ref, gt_ref, wide_l, low_l, sq_l, mix_l), (hb, gt_ref, g_ref, wide_r, low_r, sq_r, mix_r))
        bounds = []
        for first, a, b, wide, low, sq, mix in sides:
            sums = jnp.zeros((1, order), F32)
            for i, rs in enumerate(blocks):
                prev = statfull[pl.ds(first + i * (rb // 16), rb // 16)].reshape(rb, order).astype(F32)
                stat = DECAY * prev + (1.0 - DECAY) * wide_dot(a[rs, :], b[...], ((1,), (0,)))
                wide[rs, :] = stat
                sums = sums + jnp.sum(jnp.abs(stat), axis=0, keepdims=True)
            bounds.append(jnp.max(sums, axis=1, keepdims=True))
        for (first, a, b, wide, low, sq, mix), bound in zip(sides, bounds):
            scale = 1.0 / bound
            for rs in blocks:
                scaled = wide[rs, :] * scale
                wide[rs, :] = scaled
                low[rs, :] = scaled.astype(BF16)
        for first, a, b, wide, low, sq, mix in sides:
            for rs in blocks:
                square = wide_dot(low[rs, :], low[...], ((1,), (0,))).astype(BF16)
                sq[rs, :] = square
                mix[rs, :] = (square.astype(F32) - 9.0 * wide[rs, :]).astype(BF16)
        for first, a, b, wide, low, sq, mix in sides:
            for i, rs in enumerate(blocks):
                eye = (lax.broadcasted_iota(jnp.int32, (rb, order), 0) + i * rb
                       == lax.broadcasted_iota(jnp.int32, (rb, order), 1)).astype(F32)
                square = sq[rs, :]
                quartic = wide_dot(square, mix[...], ((1,), (0,)))
                low[rs, :] = (36.0 * eye - 39.0 * wide[rs, :] + 27.0 * square.astype(F32) + quartic).astype(BF16)
        grad_sum = jnp.zeros((1, order), F32)
        cond_sum = jnp.zeros((1, order), F32)
        for rs in blocks:
            done = wide_dot(low_l[rs, :], g_ref[...], ((1,), (0,))).astype(BF16)
            cond = wide_dot(done, low_r[...], ((1,), (0,)))
            wide_l[rs, :] = cond
            grad = g_ref[rs, :].astype(F32)
            grad_sum = grad_sum + jnp.sum(grad * grad, axis=0, keepdims=True)
            cond_sum = cond_sum + jnp.sum(cond * cond, axis=0, keepdims=True)
        count = 1.0 / (order * order)
        grad_power = jnp.sum(grad_sum, axis=1, keepdims=True) * count
        cond_power = jnp.sum(cond_sum, axis=1, keepdims=True) * count
        graft = jnp.sqrt(grad_power) / jnp.sqrt(cond_power + EPSILON)
        for i, rs in enumerate(blocks):
            update = wide_l[rs, :] * graft
            halves = [update[:, h * 2 * cw:(h + 1) * 2 * cw].reshape(rb // 8, 8, 2 * cw) for h in range(2)]
            upd[pl.ds(i * (rb // 8), rb // 8)] = jnp.concatenate(halves, axis=1).astype(BF16)

        @pl.loop(1, nb)
        def _(r):
            d = lax.rem(me + r, nb)
            pltpu.make_async_remote_copy(
                src_ref=upd.at[d], dst_ref=rbuf.at[own_site],
                send_sem=u_send, recv_sem=u_recv,
                device_id=there(z, d), device_id_type=MESH).start()

        rbuf[own_site] = upd[me]
        settle(rbuf.at[pl.ds(0, grp - 1)], u_recv)
        settle(upd.at[pl.ds(0, nb - 1)], u_send)

    @pl.when(jnp.logical_not(is_site))
    def _():
        settle(rbuf, u_recv)

    returned = rbuf[...].astype(F32).reshape(grp, 2, 8, 2 * cw)
    for h in range(2):
        out[:, h * 2 * cw:(h + 1) * 2 * cw] = returned[:, h].reshape(rows, 2 * cw).astype(BF16)

    settle(statbuf.at[pl.ds(0, nb - 1)], s_send)

    @pl.when(is_site)
    def _():
        settle(selbuf.at[pl.ds(0, grp - 1)], f_send)
        for w in range(2):
            settle(zstage.at[w, pl.ds(0, grp - 1)], g_send.at[w])

    @pl.when(jnp.logical_not(is_site))
    def _():
        settle(selbuf, f_send)
        for w in range(2):
            settle(zstage.at[w], g_send.at[w])

    for k in range(4):
        for way in range(2):
            first = half - arc(k, way)

            @pl.loop(first, half)
            def _(s):
                hop(zrecv.at[way, k, s], way, k, s).wait_send()


def body(grad_part, owner_table, left_stats, right_stats):
    nz, nb = lax.axis_size("dp"), lax.axis_size("block")
    grp = owner_table.shape[0]
    order = left_stats.shape[-1]
    cw, rows, half = order // 4, grp * 8, nz // 2
    vmem, dma = pltpu.VMEM, pltpu.SemaphoreType.DMA
    out = pl.pallas_call(
        functools.partial(kernel, nz, nb, grp),
        out_shape=jax.ShapeDtypeStruct((rows, order), BF16),
        in_specs=[pl.BlockSpec(memory_space=pltpu.SMEM), pl.BlockSpec(memory_space=pltpu.VMEM),
                  pl.BlockSpec(memory_space=pl.ANY), pl.BlockSpec(memory_space=pl.ANY)],
        out_specs=pl.BlockSpec(memory_space=pltpu.VMEM),
        scratch_shapes=[
            vmem((2, 4, half, rows, cw), BF16), vmem((2, grp, 16, cw), BF16), vmem((2, nb, 16, cw), BF16),
            vmem((nb, 16, order), BF16), vmem((grp, 16, order), BF16), vmem((nb, 16, order), BF16),
            vmem((order, order), BF16), vmem((order, order), BF16),
            vmem((order, order), F32), vmem((order, order), F32),
            vmem((order, order), BF16), vmem((order, order), BF16), vmem((order, order), BF16),
            vmem((order, order), BF16), vmem((order, order), BF16), vmem((order, order), BF16),
            vmem((nb, 16, 2 * cw), BF16), vmem((grp, 16, 2 * cw), BF16),
            dma((2, 4, half)), dma((2, 4, half)), dma((2,)), dma((2,)),
            dma, dma, dma, dma, dma, dma, dma,
        ],
        compiler_params=pltpu.CompilerParams(
            collective_id=0, has_side_effects=True, vmem_limit_bytes=40 * 1024 * 1024),
    )(owner_table, grad_part.reshape(nz * rows, order), left_stats[0, 0], right_stats[0, 0])
    return out.reshape(grp, 8, order)


def solution(mesh):
    placed = (
        P("dp", None, "block", None),
        P("dp"),
        P("dp", "block", None, None),
        P("dp", "block", None, None),
    )
    return jax.shard_map(
        body, mesh=mesh, in_specs=placed, out_specs=P("dp", "block", None), check_vma=False
    )
```

```python
import functools

import jax
import jax.numpy as jnp
from jax import lax
from jax.experimental import pallas as pl
from jax.experimental.pallas import tpu as pltpu
from jax.sharding import PartitionSpec as P

DECAY = 0.9
EPSILON = 1e-06
MESH = pl.DeviceIdType.MESH
F32 = jnp.float32
BF16 = jnp.bfloat16


def site_of(j):
    return 4 * j + 2 * lax.rem(j // 2, 2) + 1


def zigzag(i, n):
    return n // 2 + jnp.where(lax.rem(i, 2) == 1, -((i + 1) // 2), i // 2)


def wide_dot(a, b, contract):
    return lax.dot_general(a, b, ((contract[0], contract[1]), ((), ())), preferred_element_type=F32)


def kernel(nz, nb, grp, table, gp_hbm, left, right, out, gp, gp_sem,
           zrecv, zstage, gbuf, l_ref, r_ref, pair, statbuf, selbuf, statfull, m_ref, mt_ref,
           diag, diags, g_ref, gt_ref,
           wide_l, wide_r, low_l, low_r, sq_l, sq_r, mix_l, mix_r, upd, rbuf,
           z_send, z_recv, g_send, g_recv, s_send, s_recv, f_send, f_recv, u_send, u_recv, d_send, d_recv,
           l_sem, r_sem):
    z = lax.axis_index("dp")
    me = lax.axis_index("block")
    order = 8 * nb
    cw = order // 4
    rows = grp * 8
    half = nz // 2
    own_site = me // 4
    is_site = me == site_of(own_site)

    def there(dp, block):
        return {"dp": dp, "block": block}

    up, down = lax.rem(z + 1, nz), lax.rem(z + nz - 1, nz)
    hb = nb // 2
    load = pltpu.make_async_copy(gp_hbm, gp, gp_sem)
    load.start()
    load_l = pltpu.make_async_copy(left, l_ref, l_sem)
    load_l.start()
    load_r = pltpu.make_async_copy(right, r_ref, r_sem)
    load_r.start()

    def each_peer(low, high, act):
        if low == 0:
            act(lax.rem(me + hb, nb))
            low = 1

        @pl.loop(low, high)
        def _(i):
            act(lax.rem(me + (hb + i), nb))
            act(lax.rem(me + (hb - i), nb))

    def peer_site(i):
        return lax.rem(own_site + zigzag(i, grp), grp)

    barrier = pltpu.get_barrier_semaphore()
    for neighbour in (up, down):
        pl.semaphore_signal(barrier, inc=1, device_id=there(neighbour, me), device_id_type=MESH)

    each_peer(0, hb, lambda d: pl.semaphore_signal(
        barrier, inc=1, device_id=there(z, d), device_id_type=MESH))

    load_l.wait()
    load_r.wait()
    rb4 = order // 4
    for i in range(4):
        rs = pl.ds(i * rb4, rb4)
        row = lax.broadcasted_iota(jnp.int32, (rb4, order), 0) + i * rb4
        col = lax.broadcasted_iota(jnp.int32, (rb4, order), 1)
        right_rows = r_ref[rs, :].astype(F32)
        both = jnp.where(col >= row, l_ref[rs, :].astype(F32), right_rows).astype(BF16)
        for h in range(2):
            pair[h, rs, :] = both[:, h * 2 * cw:(h + 1) * 2 * cw]
        on_diagonal = jnp.sum(jnp.where(col == row, right_rows, 0.0), axis=0, keepdims=True)
        diag[pl.ds(i, 1), :] = on_diagonal[:, i * cw:(i + 1) * cw]
    diag[pl.ds(4, 4), :] = jnp.zeros((4, cw), F32)
    statbuf[me] = pair[me // hb, pl.ds(pl.multiple_of(16 * lax.rem(me, hb), 16), 16), :]

    @pl.when(is_site)
    def _():
        diags[me] = diag[...]

    def spread(low, high):
        def act(d):
            pltpu.make_async_remote_copy(
                src_ref=pair.at[d // hb, pl.ds(pl.multiple_of(16 * lax.rem(d, hb), 16), 16)], dst_ref=statbuf.at[me],
                send_sem=s_send, recv_sem=s_recv, device_id=there(z, d), device_id_type=MESH).start()

        each_peer(low, high, act)

    def spread_diagonal():
        @pl.loop(0, grp)
        def _(i):
            who = site_of(peer_site(i))

            @pl.when(who != me)
            def _():
                pltpu.make_async_remote_copy(
                    src_ref=diag, dst_ref=diags.at[me], send_sem=d_send, recv_sem=d_recv,
                    device_id=there(z, who), device_id_type=MESH).start()

    def column(k):
        return pl.ds(k * cw, cw)

    def own_rows(d):
        return pl.ds(pl.multiple_of(d * rows, rows), rows)

    def arc(k, way):
        return half if (k + way) % 2 == 0 else half - 1

    def hop(src, way, k, s):
        return pltpu.make_async_remote_copy(
            src_ref=src, dst_ref=zrecv.at[way, k, s],
            send_sem=z_send.at[way, k, s], recv_sem=z_recv.at[way, k, s],
            device_id=there(up if way == 0 else down, me), device_id_type=MESH)

    def target(way, dist):
        return lax.rem(z + dist, nz) if way == 0 else lax.rem(z + nz - dist, nz)

    def begin(s, ways):
        for k in range(4):
            for way in ways:
                if half - arc(k, way) == s:
                    d = target(way, half - s)
                    hop(gp.at[own_rows(d), column(k)], way, k, s).start()

    def onward(s, k, way):
        held = zrecv.at[way, k, s - 1]
        hop(held, way, k, s - 1).wait_recv()
        d = target(way, half - s)
        held[...] = (held[...].astype(F32) + gp[own_rows(d), column(k)].astype(F32)).astype(BF16)
        hop(held, way, k, s).start()

    load.wait()
    third = hb // 3

    pl.semaphore_wait(barrier, nb + 1)
    begin(0, (0, 1))
    begin(1, (0, 1))
    spread(0, third)

    for k in range(4):
        for way in range(2):
            if arc(k, way) == half:
                onward(1, k, way)

    spread(third, 2 * third)

    def all_onward(s):
        for k in range(4):
            for way in range(2):
                onward(s, k, way)

    if half > 2:
        all_onward(2)

    spread(2 * third, hb)
    spread_diagonal()

    @pl.loop(3, half)
    def _(s):
        all_onward(s)

    for w in range(2):
        parts = []
        for k in (2 * w, 2 * w + 1):
            for way in range(2):
                hop(zrecv.at[way, k, half - 1], way, k, half - 1).wait_recv()
            total = (gp[own_rows(z), column(k)].astype(F32) + zrecv[0, k, half - 1].astype(F32)
                     + zrecv[1, k, half - 1].astype(F32))
            parts.append(total.reshape(grp, 8, cw))
        zstage[w] = jnp.concatenate(parts, axis=1).astype(BF16)

        @pl.loop(0, grp)
        def _(i):
            j = peer_site(i)
            who = site_of(j)

            @pl.when(who != me)
            def _():
                pltpu.make_async_remote_copy(
                    src_ref=zstage.at[w, j], dst_ref=gbuf.at[w, me],
                    send_sem=g_send.at[w], recv_sem=g_recv.at[w],
                    device_id=there(z, who), device_id_type=MESH).start()

        @pl.when(is_site)
        def _():
            gbuf[w, me] = zstage[w, own_site]

    def settle(ref, sem):
        pltpu.make_async_copy(ref, ref, sem).wait()

    settle(statbuf.at[pl.ds(0, nb - 1)], s_recv)

    @pl.loop(0, grp)
    def _(i):
        j = peer_site(i)
        selbuf[j] = statbuf[table[j]]
        who = site_of(j)

        @pl.when(who != me)
        def _():
            pltpu.make_async_remote_copy(
                src_ref=selbuf.at[j], dst_ref=statfull.at[me],
                send_sem=f_send, recv_sem=f_recv,
                device_id=there(z, who), device_id_type=MESH).start()

    @pl.when(is_site)
    def _():
        statfull[me] = selbuf[own_site]

    @pl.when(is_site)
    def _():
        for w in range(2):
            settle(gbuf.at[w, pl.ds(0, nb - 1)], g_recv.at[w])
            pieces = gbuf[w].astype(F32).reshape(nb, 2, 8, cw)
            for h in range(2):
                piece = pieces[:, h].reshape(order, cw).astype(BF16)
                g_ref[:, column(2 * w + h)] = piece
                gt_ref[column(2 * w + h), :] = piece.T
        settle(diags.at[pl.ds(0, nb - 1)], d_recv)
        chosen = diags[table[own_site]]
        right_diag = jnp.concatenate([chosen[i:i + 1, :] for i in range(4)], axis=1)
        settle(statfull.at[pl.ds(0, nb - 1)], f_recv)
        for h in range(2):
            columns = statfull[pl.ds(h * hb, hb)].reshape(order, 2 * cw)
            m_ref[:, h * 2 * cw:(h + 1) * 2 * cw] = columns
            mt_ref[h * 2 * cw:(h + 1) * 2 * cw, :] = columns.T
        nr = 2
        rb = order // nr
        blocks = [pl.ds(i * rb, rb) for i in range(nr)]
        sides = ((0, g_ref, gt_ref, wide_l, low_l, sq_l, mix_l), (1, gt_ref, g_ref, wide_r, low_r, sq_r, mix_r))
        bounds = []
        for side, a, b, wide, low, sq, mix in sides:
            sums = jnp.zeros((1, order), F32)
            for i, rs in enumerate(blocks):
                row = lax.broadcasted_iota(jnp.int32, (rb, order), 0) + i * rb
                col = lax.broadcasted_iota(jnp.int32, (rb, order), 1)
                above, below = (m_ref, mt_ref) if side == 0 else (mt_ref, m_ref)
                prev = jnp.where(col >= row, above[rs, :].astype(F32), below[rs, :].astype(F32))
                if side == 1:
                    prev = jnp.where(col == row, right_diag, prev)
                stat = DECAY * prev + (1.0 - DECAY) * wide_dot(a[rs, :], b[...], ((1,), (0,)))
                wide[rs, :] = stat
                sums = sums + jnp.sum(jnp.abs(stat), axis=0, keepdims=True)
            bounds.append(jnp.max(sums, axis=1, keepdims=True))
        for (side, a, b, wide, low, sq, mix), bound in zip(sides, bounds):
            scale = 1.0 / bound
            for rs in blocks:
                scaled = wide[rs, :] * scale
                wide[rs, :] = scaled
                low[rs, :] = scaled.astype(BF16)
        for side, a, b, wide, low, sq, mix in sides:
            for rs in blocks:
                square = wide_dot(low[rs, :], low[...], ((1,), (0,))).astype(BF16)
                sq[rs, :] = square
                mix[rs, :] = (square.astype(F32) - 9.0 * wide[rs, :]).astype(BF16)
        for side, a, b, wide, low, sq, mix in sides:
            for i, rs in enumerate(blocks):
                eye = (lax.broadcasted_iota(jnp.int32, (rb, order), 0) + i * rb
                       == lax.broadcasted_iota(jnp.int32, (rb, order), 1)).astype(F32)
                square = sq[rs, :]
                quartic = wide_dot(square, mix[...], ((1,), (0,)))
                low[rs, :] = (36.0 * eye - 39.0 * wide[rs, :] + 27.0 * square.astype(F32) + quartic).astype(BF16)
        grad_sum = jnp.zeros((1, order), F32)
        cond_sum = jnp.zeros((1, order), F32)
        for rs in blocks:
            done = wide_dot(low_l[rs, :], g_ref[...], ((1,), (0,))).astype(BF16)
            cond = wide_dot(done, low_r[...], ((1,), (0,)))
            wide_l[rs, :] = cond
            grad = g_ref[rs, :].astype(F32)
            grad_sum = grad_sum + jnp.sum(grad * grad, axis=0, keepdims=True)
            cond_sum = cond_sum + jnp.sum(cond * cond, axis=0, keepdims=True)
        count = 1.0 / (order * order)
        grad_power = jnp.sum(grad_sum, axis=1, keepdims=True) * count
        cond_power = jnp.sum(cond_sum, axis=1, keepdims=True) * count
        graft = jnp.sqrt(grad_power) / jnp.sqrt(cond_power + EPSILON)
        for i, rs in enumerate(blocks):
            update = wide_l[rs, :] * graft
            halves = [update[:, h * 2 * cw:(h + 1) * 2 * cw].reshape(rb // 8, 8, 2 * cw) for h in range(2)]
            upd[pl.ds(i * (rb // 8), rb // 8)] = jnp.concatenate(halves, axis=1).astype(BF16)

        def send_back(d):
            pltpu.make_async_remote_copy(
                src_ref=upd.at[d], dst_ref=rbuf.at[own_site],
                send_sem=u_send, recv_sem=u_recv,
                device_id=there(z, d), device_id_type=MESH).start()

        each_peer(0, hb, send_back)
        rbuf[own_site] = upd[me]
        settle(rbuf.at[pl.ds(0, grp - 1)], u_recv)
        settle(upd.at[pl.ds(0, nb - 1)], u_send)

    @pl.when(jnp.logical_not(is_site))
    def _():
        settle(rbuf, u_recv)

    returned = rbuf[...].astype(F32).reshape(grp, 2, 8, 2 * cw)
    for h in range(2):
        out[:, h * 2 * cw:(h + 1) * 2 * cw] = returned[:, h].reshape(rows, 2 * cw).astype(BF16)

    settle(statbuf.at[pl.ds(0, nb - 1)], s_send)

    @pl.when(is_site)
    def _():
        settle(selbuf.at[pl.ds(0, grp - 1)], f_send)
        settle(diags.at[pl.ds(0, grp - 1)], d_send)
        for w in range(2):
            settle(zstage.at[w, pl.ds(0, grp - 1)], g_send.at[w])

    @pl.when(jnp.logical_not(is_site))
    def _():
        settle(selbuf, f_send)
        settle(diags.at[pl.ds(0, grp)], d_send)
        for w in range(2):
            settle(zstage.at[w], g_send.at[w])

    for k in range(4):
        for way in range(2):
            first = half - arc(k, way)

            @pl.loop(first, half)
            def _(s):
                hop(zrecv.at[way, k, s], way, k, s).wait_send()


def body(grad_part, owner_table, left_stats, right_stats):
    nz, nb = lax.axis_size("dp"), lax.axis_size("block")
    grp = owner_table.shape[0]
    order = left_stats.shape[-1]
    cw, rows, half = order // 4, grp * 8, nz // 2
    vmem, dma = pltpu.VMEM, pltpu.SemaphoreType.DMA
    out = pl.pallas_call(
        functools.partial(kernel, nz, nb, grp),
        out_shape=jax.ShapeDtypeStruct((rows, order), BF16),
        in_specs=[pl.BlockSpec(memory_space=pltpu.SMEM), pl.BlockSpec(memory_space=pltpu.HBM),
                  pl.BlockSpec(memory_space=pltpu.HBM), pl.BlockSpec(memory_space=pltpu.HBM)],
        out_specs=pl.BlockSpec(memory_space=pltpu.VMEM),
        scratch_shapes=[vmem((nz * rows, order), BF16), dma,
            vmem((2, 4, half, rows, cw), BF16), vmem((2, grp, 16, cw), BF16), vmem((2, nb, 16, cw), BF16),
            vmem((order, order), BF16), vmem((order, order), BF16), vmem((2, order, 2 * cw), BF16),
            vmem((nb, 16, 2 * cw), BF16), vmem((grp, 16, 2 * cw), BF16), vmem((nb, 16, 2 * cw), BF16),
            vmem((order, order), BF16), vmem((order, order), BF16),
            vmem((8, cw), F32), vmem((nb, 8, cw), F32),
            vmem((order, order), BF16), vmem((order, order), BF16),
            vmem((order, order), F32), vmem((order, order), F32),
            vmem((order, order), BF16), vmem((order, order), BF16), vmem((order, order), BF16),
            vmem((order, order), BF16), vmem((order, order), BF16), vmem((order, order), BF16),
            vmem((nb, 16, 2 * cw), BF16), vmem((grp, 16, 2 * cw), BF16),
            dma((2, 4, half)), dma((2, 4, half)), dma((2,)), dma((2,)),
            dma, dma, dma, dma, dma, dma, dma, dma, dma, dma,
        ],
        compiler_params=pltpu.CompilerParams(
            collective_id=0, has_side_effects=True, vmem_limit_bytes=62 * 1024 * 1024),
    )(owner_table, grad_part.reshape(nz * rows, order), left_stats[0, 0], right_stats[0, 0])
    return out.reshape(grp, 8, order)


def solution(mesh):
    placed = (
        P("dp", None, "block", None),
        P("dp"),
        P("dp", "block", None, None),
        P("dp", "block", None, None),
    )
    return jax.shard_map(
        body, mesh=mesh, in_specs=placed, out_specs=P("dp", "block", None), check_vma=False
    )
```

```python
import functools

import jax
import jax.numpy as jnp
from jax import lax
from jax.experimental import pallas as pl
from jax.experimental.pallas import tpu as pltpu
from jax.sharding import PartitionSpec as P

DECAY = 0.9
EPSILON = 1e-06
MESH = pl.DeviceIdType.MESH
F32 = jnp.float32
BF16 = jnp.bfloat16


def site_of(j):
    return 4 * j + 2 * lax.rem(j // 2, 2) + 1


def zigzag(i, n):
    return n // 2 + jnp.where(lax.rem(i, 2) == 1, -((i + 1) // 2), i // 2)


def wide_dot(a, b, contract):
    return lax.dot_general(a, b, ((contract[0], contract[1]), ((), ())), preferred_element_type=F32)


def kernel(nz, nb, grp, table, gp_hbm, left, right, out, gp, gp_sem,
           zrecv, zstage, gbuf, l_ref, r_ref, pair, statbuf, selbuf, statfull, m_ref, mt_ref,
           diag, diags, g_ref, gt_ref,
           wide_l, wide_r, low_l, low_r, sq_l, sq_r, mix_l, mix_r, upd, rbuf,
           z_send, z_recv, g_send, g_recv, s_send, s_recv, f_send, f_recv, u_send, u_recv, d_send, d_recv,
           l_sem, r_sem, ready, token):
    z = lax.axis_index("dp")
    me = lax.axis_index("block")
    order = 8 * nb
    cw = order // 4
    rows = grp * 8
    half = nz // 2
    own_site = me // 4
    is_site = me == site_of(own_site)

    def there(dp, block):
        return {"dp": dp, "block": block}

    up, down = lax.rem(z + 1, nz), lax.rem(z + nz - 1, nz)
    hb = nb // 2
    load = pltpu.make_async_copy(gp_hbm, gp, gp_sem)
    load.start()
    load_l = pltpu.make_async_copy(left, l_ref, l_sem)
    load_l.start()
    load_r = pltpu.make_async_copy(right, r_ref, r_sem)
    load_r.start()

    def each_peer(low, high, act):
        if low == 0:
            act(lax.rem(me + hb, nb))
            low = 1

        @pl.loop(low, high)
        def _(i):
            act(lax.rem(me + (hb + i), nb))
            act(lax.rem(me + (hb - i), nb))

    def peer_site(i):
        return lax.rem(own_site + zigzag(i, grp), grp)

    cores, width = 2, 4
    height = nb // (cores * width)
    y, x, c = me // (cores * width), lax.rem(me // cores, width), lax.rem(me, cores)

    def moved(dy, dx, dc):
        return (lax.rem(y + dy + height, height) * width + lax.rem(x + dx + width, width)) * cores + lax.rem(c + dc, cores)

    first_plane = z == 0
    late = z >= half
    barrier = pltpu.get_barrier_semaphore()

    def tell(semaphore, dp, block):
        pl.semaphore_signal(semaphore, inc=1, device_id=there(dp, block), device_id_type=MESH)

    for neighbour in (up, down):
        @pl.when(neighbour != 0)
        def _():
            tell(barrier, neighbour, me)

    @pl.when(late)
    def _():
        for dy, dx, dc in ((1, 0, 0), (-1, 0, 0), (0, 1, 0), (0, -1, 0), (0, 0, 1)):
            tell(barrier, z, moved(dy, dx, dc))

    @pl.when(jnp.logical_not(late))
    def _():
        each_peer(0, hb, lambda d: tell(barrier, z, d))

    rounds = [((1, 0, 0), (-1, 0, 0), (0, 0, 1)),
              ((2, 0, 0), (-2, 0, 0)) if height > 4 else (),
              ((0, 1, 0), (0, -1, 0), (0, 1, 1), (0, -1, 1), (0, 0, 1)),
              ((0, 2, 0), (0, 2, 1))]

    def give(r):
        @pl.when(late)
        def _():
            for step in rounds[r]:
                tell(token.at[r], z, moved(*step))

    def take(r):
        @pl.when(late)
        def _():
            if rounds[r]:
                pl.semaphore_wait(token.at[r], len(rounds[r]))

    load_l.wait()
    load_r.wait()
    rb4 = order // 4
    for i in range(4):
        rs = pl.ds(i * rb4, rb4)
        row = lax.broadcasted_iota(jnp.int32, (rb4, order), 0) + i * rb4
        col = lax.broadcasted_iota(jnp.int32, (rb4, order), 1)
        right_rows = r_ref[rs, :].astype(F32)
        both = jnp.where(col >= row, l_ref[rs, :].astype(F32), right_rows).astype(BF16)
        for h in range(2):
            pair[h, rs, :] = both[:, h * 2 * cw:(h + 1) * 2 * cw]
        on_diagonal = jnp.sum(jnp.where(col == row, right_rows, 0.0), axis=0, keepdims=True)
        diag[pl.ds(i, 1), :] = on_diagonal[:, i * cw:(i + 1) * cw]
    diag[pl.ds(4, 4), :] = jnp.zeros((4, cw), F32)
    statbuf[me] = pair[me // hb, pl.ds(pl.multiple_of(16 * lax.rem(me, hb), 16), 16), :]

    @pl.when(is_site)
    def _():
        diags[me] = diag[...]

    def spread(low, high):
        def act(d):
            pltpu.make_async_remote_copy(
                src_ref=pair.at[d // hb, pl.ds(pl.multiple_of(16 * lax.rem(d, hb), 16), 16)], dst_ref=statbuf.at[me],
                send_sem=s_send, recv_sem=s_recv, device_id=there(z, d), device_id_type=MESH).start()

        each_peer(low, high, act)

    def spread_diagonal():
        @pl.loop(0, grp)
        def _(i):
            who = site_of(peer_site(i))

            @pl.when(who != me)
            def _():
                pltpu.make_async_remote_copy(
                    src_ref=diag, dst_ref=diags.at[me], send_sem=d_send, recv_sem=d_recv,
                    device_id=there(z, who), device_id_type=MESH).start()

    part = rows // 4

    def own_part(d, k):
        return gp.at[pl.ds(pl.multiple_of(d * rows + k * part, part), part), :]

    def arc(k, way):
        return half if (k + way) % 2 == 0 else half - 1

    def hop(src, way, k, s):
        return pltpu.make_async_remote_copy(
            src_ref=src, dst_ref=zrecv.at[way, k, s],
            send_sem=z_send.at[way, k, s], recv_sem=z_recv.at[way, k, s],
            device_id=there(up if way == 0 else down, me), device_id_type=MESH)

    def target(way, dist):
        return lax.rem(z + dist, nz) if way == 0 else lax.rem(z + nz - dist, nz)

    def begin(s, ways):
        for k in range(4):
            for way in ways:
                if half - arc(k, way) == s:
                    d = target(way, half - s)
                    hop(own_part(d, k), way, k, s).start()

    def onward(s, k, way):
        held = zrecv.at[way, k, s - 1]
        hop(held, way, k, s - 1).wait_recv()
        d = target(way, half - s)
        held[...] = (held[...].astype(F32) + own_part(d, k)[...].astype(F32)).astype(BF16)
        hop(held, way, k, s).start()

    load.wait()
    third = hb // 3

    @pl.when(first_plane)
    def _():
        pl.semaphore_wait(barrier, nb - 1)
        spread(0, hb)
        spread_diagonal()
        for way in range(2):
            pl.semaphore_wait(ready.at[way], 1)
            begin(0, (way,))
            begin(1, (way,))

    @pl.when(jnp.logical_not(first_plane))
    def _():
        @pl.when(late)
        def _():
            pl.semaphore_wait(barrier, 7)

        @pl.when(jnp.logical_not(late))
        def _():
            pl.semaphore_wait(barrier, nb + 1)

        for way, neighbour in ((1, up), (0, down)):
            @pl.when(neighbour == 0)
            def _():
                tell(ready.at[way], 0, me)

        begin(0, (0, 1))
        begin(1, (0, 1))

        @pl.when(jnp.logical_not(late))
        def _():
            spread(0, third)

    give(0)
    take(0)
    give(1)
    for k in range(4):
        for way in range(2):
            if arc(k, way) == half:
                onward(1, k, way)
    take(1)
    give(2)

    early = jnp.logical_and(jnp.logical_not(late), jnp.logical_not(first_plane))

    @pl.when(early)
    def _():
        spread(third, 2 * third)

    def some_onward(s, low, high):
        for k in range(low, high):
            for way in range(2):
                onward(s, k, way)

    if half > 2:
        some_onward(2, 0, 2)
    take(2)
    give(3)
    if half > 2:
        some_onward(2, 2, 4)
    take(3)

    @pl.when(early)
    def _():
        spread(2 * third, hb)
        spread_diagonal()

    @pl.when(late)
    def _():
        spread(0, 2 * third)

    if half > 3:
        some_onward(3, 0, 4)

    @pl.when(late)
    def _():
        spread(2 * third, hb)
        spread_diagonal()

    @pl.loop(4, half)
    def _(s):
        some_onward(s, 0, 4)

    few = grp // 4
    for k in range(4):
        total = own_part(z, k)[...].astype(F32)
        for way in range(2):
            hop(zrecv.at[way, k, half - 1], way, k, half - 1).wait_recv()
            total = total + zrecv[way, k, half - 1].astype(F32)
        halves = [total[:, h * 2 * cw:(h + 1) * 2 * cw].reshape(few, 8, 2 * cw) for h in range(2)]
        zstage[pl.ds(k * few, few)] = jnp.concatenate(halves, axis=1).astype(BF16)

        @pl.loop(k * few, (k + 1) * few)
        def _(j):
            who = site_of(j)

            @pl.when(who != me)
            def _():
                pltpu.make_async_remote_copy(
                    src_ref=zstage.at[j], dst_ref=gbuf.at[me], send_sem=g_send, recv_sem=g_recv,
                    device_id=there(z, who), device_id_type=MESH).start()

            @pl.when(who == me)
            def _():
                gbuf[me] = zstage[j]

    def settle(ref, sem):
        pltpu.make_async_copy(ref, ref, sem).wait()

    settle(statbuf.at[pl.ds(0, nb - 1)], s_recv)

    @pl.loop(0, grp)
    def _(i):
        j = peer_site(i)
        selbuf[j] = statbuf[table[j]]
        who = site_of(j)

        @pl.when(who != me)
        def _():
            pltpu.make_async_remote_copy(
                src_ref=selbuf.at[j], dst_ref=statfull.at[me],
                send_sem=f_send, recv_sem=f_recv,
                device_id=there(z, who), device_id_type=MESH).start()

    @pl.when(is_site)
    def _():
        statfull[me] = selbuf[own_site]

    @pl.when(is_site)
    def _():
        settle(gbuf.at[pl.ds(0, nb - 1)], g_recv)
        pieces = gbuf[...].astype(F32).reshape(nb, 2, 8, 2 * cw)
        for h in range(2):
            piece = pieces[:, h].reshape(order, 2 * cw).astype(BF16)
            g_ref[:, h * 2 * cw:(h + 1) * 2 * cw] = piece
            gt_ref[h * 2 * cw:(h + 1) * 2 * cw, :] = piece.T
        settle(diags.at[pl.ds(0, nb - 1)], d_recv)
        chosen = diags[table[own_site]]
        right_diag = jnp.concatenate([chosen[i:i + 1, :] for i in range(4)], axis=1)
        settle(statfull.at[pl.ds(0, nb - 1)], f_recv)
        for h in range(2):
            columns = statfull[pl.ds(h * hb, hb)].reshape(order, 2 * cw)
            m_ref[:, h * 2 * cw:(h + 1) * 2 * cw] = columns
            mt_ref[h * 2 * cw:(h + 1) * 2 * cw, :] = columns.T
        nr = 2
        rb = order // nr
        blocks = [pl.ds(i * rb, rb) for i in range(nr)]
        sides = ((0, g_ref, gt_ref, wide_l, low_l, sq_l, mix_l), (1, gt_ref, g_ref, wide_r, low_r, sq_r, mix_r))
        bounds = []
        for side, a, b, wide, low, sq, mix in sides:
            sums = jnp.zeros((1, order), F32)
            for i, rs in enumerate(blocks):
                row = lax.broadcasted_iota(jnp.int32, (rb, order), 0) + i * rb
                col = lax.broadcasted_iota(jnp.int32, (rb, order), 1)
                above, below = (m_ref, mt_ref) if side == 0 else (mt_ref, m_ref)
                prev = jnp.where(col >= row, above[rs, :].astype(F32), below[rs, :].astype(F32))
                if side == 1:
                    prev = jnp.where(col == row, right_diag, prev)
                stat = DECAY * prev + (1.0 - DECAY) * wide_dot(a[rs, :], b[...], ((1,), (0,)))
                wide[rs, :] = stat
                sums = sums + jnp.sum(jnp.abs(stat), axis=0, keepdims=True)
            bounds.append(jnp.max(sums, axis=1, keepdims=True))
        for (side, a, b, wide, low, sq, mix), bound in zip(sides, bounds):
            scale = 1.0 / bound
            for rs in blocks:
                scaled = wide[rs, :] * scale
                wide[rs, :] = scaled
                low[rs, :] = scaled.astype(BF16)
        for side, a, b, wide, low, sq, mix in sides:
            for rs in blocks:
                square = wide_dot(low[rs, :], low[...], ((1,), (0,))).astype(BF16)
                sq[rs, :] = square
                mix[rs, :] = (square.astype(F32) - 9.0 * wide[rs, :]).astype(BF16)
        for side, a, b, wide, low, sq, mix in sides:
            for i, rs in enumerate(blocks):
                eye = (lax.broadcasted_iota(jnp.int32, (rb, order), 0) + i * rb
                       == lax.broadcasted_iota(jnp.int32, (rb, order), 1)).astype(F32)
                square = sq[rs, :]
                quartic = wide_dot(square, mix[...], ((1,), (0,)))
                low[rs, :] = (36.0 * eye - 39.0 * wide[rs, :] + 27.0 * square.astype(F32) + quartic).astype(BF16)
        grad_sum = jnp.zeros((1, order), F32)
        cond_sum = jnp.zeros((1, order), F32)
        for rs in blocks:
            done = wide_dot(low_l[rs, :], g_ref[...], ((1,), (0,))).astype(BF16)
            cond = wide_dot(done, low_r[...], ((1,), (0,)))
            wide_l[rs, :] = cond
            grad = g_ref[rs, :].astype(F32)
            grad_sum = grad_sum + jnp.sum(grad * grad, axis=0, keepdims=True)
            cond_sum = cond_sum + jnp.sum(cond * cond, axis=0, keepdims=True)
        count = 1.0 / (order * order)
        grad_power = jnp.sum(grad_sum, axis=1, keepdims=True) * count
        cond_power = jnp.sum(cond_sum, axis=1, keepdims=True) * count
        graft = jnp.sqrt(grad_power) / jnp.sqrt(cond_power + EPSILON)
        for i, rs in enumerate(blocks):
            update = wide_l[rs, :] * graft
            halves = [update[:, h * 2 * cw:(h + 1) * 2 * cw].reshape(rb // 8, 8, 2 * cw) for h in range(2)]
            upd[pl.ds(i * (rb // 8), rb // 8)] = jnp.concatenate(halves, axis=1).astype(BF16)

        def send_back(d):
            pltpu.make_async_remote_copy(
                src_ref=upd.at[d], dst_ref=rbuf.at[own_site],
                send_sem=u_send, recv_sem=u_recv,
                device_id=there(z, d), device_id_type=MESH).start()

        each_peer(0, hb, send_back)
        rbuf[own_site] = upd[me]
        settle(rbuf.at[pl.ds(0, grp - 1)], u_recv)
        settle(upd.at[pl.ds(0, nb - 1)], u_send)

    @pl.when(jnp.logical_not(is_site))
    def _():
        settle(rbuf, u_recv)

    returned = rbuf[...].astype(F32).reshape(grp, 2, 8, 2 * cw)
    for h in range(2):
        out[:, h * 2 * cw:(h + 1) * 2 * cw] = returned[:, h].reshape(rows, 2 * cw).astype(BF16)

    settle(statbuf.at[pl.ds(0, nb - 1)], s_send)

    @pl.when(is_site)
    def _():
        settle(selbuf.at[pl.ds(0, grp - 1)], f_send)
        settle(diags.at[pl.ds(0, grp - 1)], d_send)
        settle(zstage.at[pl.ds(0, grp - 1)], g_send)

    @pl.when(jnp.logical_not(is_site))
    def _():
        settle(selbuf, f_send)
        settle(diags.at[pl.ds(0, grp)], d_send)
        settle(zstage, g_send)

    for k in range(4):
        for way in range(2):
            first = half - arc(k, way)

            @pl.loop(first, half)
            def _(s):
                hop(zrecv.at[way, k, s], way, k, s).wait_send()


def body(grad_part, owner_table, left_stats, right_stats):
    nz, nb = lax.axis_size("dp"), lax.axis_size("block")
    grp = owner_table.shape[0]
    order = left_stats.shape[-1]
    cw, rows, half = order // 4, grp * 8, nz // 2
    vmem, dma = pltpu.VMEM, pltpu.SemaphoreType.DMA
    out = pl.pallas_call(
        functools.partial(kernel, nz, nb, grp),
        out_shape=jax.ShapeDtypeStruct((rows, order), BF16),
        in_specs=[pl.BlockSpec(memory_space=pltpu.SMEM), pl.BlockSpec(memory_space=pltpu.HBM),
                  pl.BlockSpec(memory_space=pltpu.HBM), pl.BlockSpec(memory_space=pltpu.HBM)],
        out_specs=pl.BlockSpec(memory_space=pltpu.VMEM),
        scratch_shapes=[vmem((nz * rows, order), BF16), dma,
            vmem((2, 4, half, rows // 4, order), BF16), vmem((grp, 16, 2 * cw), BF16), vmem((nb, 16, 2 * cw), BF16),
            vmem((order, order), BF16), vmem((order, order), BF16), vmem((2, order, 2 * cw), BF16),
            vmem((nb, 16, 2 * cw), BF16), vmem((grp, 16, 2 * cw), BF16), vmem((nb, 16, 2 * cw), BF16),
            vmem((order, order), BF16), vmem((order, order), BF16),
            vmem((8, cw), F32), vmem((nb, 8, cw), F32),
            vmem((order, order), BF16), vmem((order, order), BF16),
            vmem((order, order), F32), vmem((order, order), F32),
            vmem((order, order), BF16), vmem((order, order), BF16), vmem((order, order), BF16),
            vmem((order, order), BF16), vmem((order, order), BF16), vmem((order, order), BF16),
            vmem((nb, 16, 2 * cw), BF16), vmem((grp, 16, 2 * cw), BF16),
            dma((2, 4, half)), dma((2, 4, half)), dma, dma,
            dma, dma, dma, dma, dma, dma, dma, dma, dma, dma,
            pltpu.SemaphoreType.REGULAR((2,)), pltpu.SemaphoreType.REGULAR((4,)),
        ],
        compiler_params=pltpu.CompilerParams(
            collective_id=0, has_side_effects=True, vmem_limit_bytes=53 * 1024 * 1024 + 512 * 1024),
    )(owner_table, grad_part.reshape(nz * rows, order), left_stats[0, 0], right_stats[0, 0])
    return out.reshape(grp, 8, order)


def solution(mesh):
    placed = (
        P("dp", None, "block", None),
        P("dp"),
        P("dp", "block", None, None),
        P("dp", "block", None, None),
    )
    return jax.shard_map(
        body, mesh=mesh, in_specs=placed, out_specs=P("dp", "block", None), check_vma=False
    )
```

```python
import functools

import jax
import jax.numpy as jnp
from jax import lax
from jax.experimental import pallas as pl
from jax.experimental.pallas import tpu as pltpu
from jax.sharding import PartitionSpec as P

DECAY = 0.9
EPSILON = 1e-06
MESH = pl.DeviceIdType.MESH
F32 = jnp.float32
BF16 = jnp.bfloat16


def site_of(j):
    return 4 * j + 2 * lax.rem(j // 2, 2) + 1


def zigzag(i, n):
    return n // 2 + jnp.where(lax.rem(i, 2) == 1, -((i + 1) // 2), i // 2)


def wide_dot(a, b, contract):
    return lax.dot_general(a, b, ((contract[0], contract[1]), ((), ())), preferred_element_type=F32)


def kernel(nz, nb, grp, table, gp_hbm, left, right, out, gp, gp_sem,
           zrecv, zstage, gbuf, l_ref, r_ref, pair, statbuf, selbuf, statfull, m_ref, mt_ref,
           diag, diags, g_ref, gt_ref,
           wide_l, wide_r, low_l, low_r, sq_l, sq_r, mix_l, mix_r, upd, rbuf,
           z_send, z_recv, g_send, g_recv, s_send, s_recv, f_send, f_recv, u_send, u_recv, d_send, d_recv,
           l_sem, r_sem, token):
    z = lax.axis_index("dp")
    me = lax.axis_index("block")
    order = 8 * nb
    cw = order // 4
    rows = grp * 8
    half = nz // 2
    own_site = me // 4
    is_site = me == site_of(own_site)

    def there(dp, block):
        return {"dp": dp, "block": block}

    up, down = lax.rem(z + 1, nz), lax.rem(z + nz - 1, nz)
    hb = nb // 2
    load = pltpu.make_async_copy(gp_hbm, gp, gp_sem)
    load.start()
    load_l = pltpu.make_async_copy(left, l_ref, l_sem)
    load_l.start()
    load_r = pltpu.make_async_copy(right, r_ref, r_sem)
    load_r.start()

    def each_peer(low, high, act):
        if low == 0:
            act(lax.rem(me + hb, nb))
            low = 1

        @pl.loop(low, high)
        def _(i):
            act(lax.rem(me + (hb + i), nb))
            act(lax.rem(me + (hb - i), nb))

    def peer_site(i):
        return lax.rem(own_site + zigzag(i, grp), grp)

    cores, width = 2, 4
    height = nb // (cores * width)
    y, x, c = me // (cores * width), lax.rem(me // cores, width), lax.rem(me, cores)

    def moved(dy, dx, dc):
        return (lax.rem(y + dy + height, height) * width + lax.rem(x + dx + width, width)) * cores + lax.rem(c + dc, cores)

    late = z >= half
    barrier = pltpu.get_barrier_semaphore()

    def tell(semaphore, dp, block):
        pl.semaphore_signal(semaphore, inc=1, device_id=there(dp, block), device_id_type=MESH)

    for neighbour in (up, down):
        tell(barrier, neighbour, me)

    @pl.when(late)
    def _():
        for dy, dx, dc in ((1, 0, 0), (-1, 0, 0), (0, 1, 0), (0, -1, 0), (0, 0, 1)):
            tell(barrier, z, moved(dy, dx, dc))

    @pl.when(jnp.logical_not(late))
    def _():
        each_peer(0, hb, lambda d: tell(barrier, z, d))

    rounds = [((1, 0, 0), (-1, 0, 0), (0, 0, 1)),
              ((2, 0, 0), (-2, 0, 0)) if height > 4 else (),
              ((0, 1, 0), (0, -1, 0), (0, 1, 1), (0, -1, 1), (0, 0, 1)),
              ((0, 2, 0), (0, 2, 1))]

    def give(r):
        @pl.when(late)
        def _():
            for step in rounds[r]:
                tell(token.at[r], z, moved(*step))

    def take(r):
        @pl.when(late)
        def _():
            if rounds[r]:
                pl.semaphore_wait(token.at[r], len(rounds[r]))

    def spread(low, high):
        def act(d):
            pltpu.make_async_remote_copy(
                src_ref=pair.at[d // hb, pl.ds(pl.multiple_of(16 * lax.rem(d, hb), 16), 16)], dst_ref=statbuf.at[me],
                send_sem=s_send, recv_sem=s_recv, device_id=there(z, d), device_id_type=MESH).start()

        each_peer(low, high, act)

    def spread_diagonal():
        @pl.loop(0, grp)
        def _(i):
            who = site_of(peer_site(i))

            @pl.when(who != me)
            def _():
                pltpu.make_async_remote_copy(
                    src_ref=diag, dst_ref=diags.at[me], send_sem=d_send, recv_sem=d_recv,
                    device_id=there(z, who), device_id_type=MESH).start()

    part = rows // 4

    def own_part(d, k, held=gp):
        return held.at[pl.ds(pl.multiple_of(d * rows + k * part, part), part), :]

    def arc(k, way):
        return half if (k + way) % 2 == 0 else half - 1

    def hop(src, way, k, s):
        return pltpu.make_async_remote_copy(
            src_ref=src, dst_ref=zrecv.at[way, k, s],
            send_sem=z_send.at[way, k, s], recv_sem=z_recv.at[way, k, s],
            device_id=there(up if way == 0 else down, me), device_id_type=MESH)

    def target(way, dist):
        return lax.rem(z + dist, nz) if way == 0 else lax.rem(z + nz - dist, nz)

    def begin(s, ways):
        for k in range(4):
            for way in ways:
                if half - arc(k, way) == s:
                    d = target(way, half - s)
                    hop(own_part(d, k, gp_hbm), way, k, s).start()

    def onward(s, k, way):
        held = zrecv.at[way, k, s - 1]
        hop(held, way, k, s - 1).wait_recv()
        d = target(way, half - s)
        held[...] = (held[...].astype(F32) + own_part(d, k)[...].astype(F32)).astype(BF16)
        hop(held, way, k, s).start()

    def settle(ref, sem):
        pltpu.make_async_copy(ref, ref, sem).wait()

    def relay():
        settle(statbuf.at[pl.ds(0, nb - 1)], s_recv)

        @pl.loop(0, grp)
        def _(i):
            j = peer_site(i)
            selbuf[j] = statbuf[table[j]]
            who = site_of(j)

            @pl.when(who != me)
            def _():
                pltpu.make_async_remote_copy(
                    src_ref=selbuf.at[j], dst_ref=statfull.at[me],
                    send_sem=f_send, recv_sem=f_recv,
                    device_id=there(z, who), device_id_type=MESH).start()

        @pl.when(is_site)
        def _():
            statfull[me] = selbuf[own_site]

    third = hb // 3

    @pl.when(late)
    def _():
        pl.semaphore_wait(barrier, 7)

    @pl.when(jnp.logical_not(late))
    def _():
        pl.semaphore_wait(barrier, nb + 1)

    begin(0, (0, 1))
    begin(1, (0, 1))
    give(0)

    load_l.wait()
    load_r.wait()
    rb4 = order // 4
    for i in range(4):
        rs = pl.ds(i * rb4, rb4)
        row = lax.broadcasted_iota(jnp.int32, (rb4, order), 0) + i * rb4
        col = lax.broadcasted_iota(jnp.int32, (rb4, order), 1)
        right_rows = r_ref[rs, :].astype(F32)
        both = jnp.where(col >= row, l_ref[rs, :].astype(F32), right_rows).astype(BF16)
        for h in range(2):
            pair[h, rs, :] = both[:, h * 2 * cw:(h + 1) * 2 * cw]
        on_diagonal = jnp.sum(jnp.where(col == row, right_rows, 0.0), axis=0, keepdims=True)
        diag[pl.ds(i, 1), :] = on_diagonal[:, i * cw:(i + 1) * cw]
    diag[pl.ds(4, 4), :] = jnp.zeros((4, cw), F32)
    statbuf[me] = pair[me // hb, pl.ds(pl.multiple_of(16 * lax.rem(me, hb), 16), 16), :]

    @pl.when(is_site)
    def _():
        diags[me] = diag[...]

    @pl.when(jnp.logical_not(late))
    def _():
        spread(0, hb)
        spread_diagonal()

    load.wait()
    take(0)
    give(1)
    for k in range(4):
        for way in range(2):
            if arc(k, way) == half:
                onward(1, k, way)
    take(1)
    give(2)

    def some_onward(s, low, high):
        for k in range(low, high):
            for way in range(2):
                onward(s, k, way)

    if half > 2:
        some_onward(2, 0, 2)
    take(2)
    give(3)
    if half > 2:
        some_onward(2, 2, 4)
    take(3)

    @pl.when(late)
    def _():
        spread(0, 2 * third)

    if half > 3:
        some_onward(3, 0, 4)

    @pl.when(late)
    def _():
        spread(2 * third, hb)
        spread_diagonal()

    @pl.loop(4, half - 1)
    def _(s):
        some_onward(s, 0, 4)

    @pl.when(jnp.logical_not(late))
    def _():
        relay()

    if half > 4:
        some_onward(half - 1, 0, 4)

    few = grp // 4
    for k in range(4):
        total = own_part(z, k)[...].astype(F32)
        for way in range(2):
            hop(zrecv.at[way, k, half - 1], way, k, half - 1).wait_recv()
            total = total + zrecv[way, k, half - 1].astype(F32)
        halves = [total[:, h * 2 * cw:(h + 1) * 2 * cw].reshape(few, 8, 2 * cw) for h in range(2)]
        zstage[pl.ds(k * few, few)] = jnp.concatenate(halves, axis=1).astype(BF16)

        @pl.loop(k * few, (k + 1) * few)
        def _(j):
            who = site_of(j)

            @pl.when(who != me)
            def _():
                pltpu.make_async_remote_copy(
                    src_ref=zstage.at[j], dst_ref=gbuf.at[me], send_sem=g_send, recv_sem=g_recv,
                    device_id=there(z, who), device_id_type=MESH).start()

            @pl.when(who == me)
            def _():
                gbuf[me] = zstage[j]

    @pl.when(late)
    def _():
        relay()

    @pl.when(is_site)
    def _():
        settle(diags.at[pl.ds(0, nb - 1)], d_recv)
        chosen = diags[table[own_site]]
        right_diag = jnp.concatenate([chosen[i:i + 1, :] for i in range(4)], axis=1)
        settle(statfull.at[pl.ds(0, nb - 1)], f_recv)
        for h in range(2):
            columns = statfull[pl.ds(h * hb, hb)].reshape(order, 2 * cw)
            m_ref[:, h * 2 * cw:(h + 1) * 2 * cw] = columns
            mt_ref[h * 2 * cw:(h + 1) * 2 * cw, :] = columns.T
        nr = 2
        rb = order // nr
        blocks = [pl.ds(i * rb, rb) for i in range(nr)]
        for i, rs in enumerate(blocks):
            row = lax.broadcasted_iota(jnp.int32, (rb, order), 0) + i * rb
            col = lax.broadcasted_iota(jnp.int32, (rb, order), 1)
            stored, turned = m_ref[rs, :].astype(F32), mt_ref[rs, :].astype(F32)
            wide_l[rs, :] = DECAY * jnp.where(col >= row, stored, turned)
            wide_r[rs, :] = DECAY * jnp.where(col == row, right_diag, jnp.where(col > row, turned, stored))
        settle(gbuf.at[pl.ds(0, nb - 1)], g_recv)
        pieces = gbuf[...].astype(F32).reshape(nb, 2, 8, 2 * cw)
        for h in range(2):
            piece = pieces[:, h].reshape(order, 2 * cw).astype(BF16)
            g_ref[:, h * 2 * cw:(h + 1) * 2 * cw] = piece
            gt_ref[h * 2 * cw:(h + 1) * 2 * cw, :] = piece.T
        sides = ((0, g_ref, gt_ref, wide_l, low_l, sq_l, mix_l), (1, gt_ref, g_ref, wide_r, low_r, sq_r, mix_r))
        bounds = []
        for side, a, b, wide, low, sq, mix in sides:
            sums = jnp.zeros((1, order), F32)
            for i, rs in enumerate(blocks):
                stat = wide[rs, :] + (1.0 - DECAY) * wide_dot(a[rs, :], b[...], ((1,), (0,)))
                wide[rs, :] = stat
                sums = sums + jnp.sum(jnp.abs(stat), axis=0, keepdims=True)
            bounds.append(jnp.max(sums, axis=1, keepdims=True))
        for (side, a, b, wide, low, sq, mix), bound in zip(sides, bounds):
            scale = 1.0 / bound
            for rs in blocks:
                scaled = wide[rs, :] * scale
                wide[rs, :] = scaled
                low[rs, :] = scaled.astype(BF16)
        for side, a, b, wide, low, sq, mix in sides:
            for rs in blocks:
                square = wide_dot(low[rs, :], low[...], ((1,), (0,))).astype(BF16)
                sq[rs, :] = square
                mix[rs, :] = (square.astype(F32) - 9.0 * wide[rs, :]).astype(BF16)
        for side, a, b, wide, low, sq, mix in sides:
            for i, rs in enumerate(blocks):
                eye = (lax.broadcasted_iota(jnp.int32, (rb, order), 0) + i * rb
                       == lax.broadcasted_iota(jnp.int32, (rb, order), 1)).astype(F32)
                square = sq[rs, :]
                quartic = wide_dot(square, mix[...], ((1,), (0,)))
                low[rs, :] = (36.0 * eye - 39.0 * wide[rs, :] + 27.0 * square.astype(F32) + quartic).astype(BF16)
        grad_sum = jnp.zeros((1, order), F32)
        cond_sum = jnp.zeros((1, order), F32)
        for rs in blocks:
            done = wide_dot(low_l[rs, :], g_ref[...], ((1,), (0,))).astype(BF16)
            cond = wide_dot(done, low_r[...], ((1,), (0,)))
            wide_l[rs, :] = cond
            grad = g_ref[rs, :].astype(F32)
            grad_sum = grad_sum + jnp.sum(grad * grad, axis=0, keepdims=True)
            cond_sum = cond_sum + jnp.sum(cond * cond, axis=0, keepdims=True)
        count = 1.0 / (order * order)
        grad_power = jnp.sum(grad_sum, axis=1, keepdims=True) * count
        cond_power = jnp.sum(cond_sum, axis=1, keepdims=True) * count
        graft = jnp.sqrt(grad_power) / jnp.sqrt(cond_power + EPSILON)
        for i, rs in enumerate(blocks):
            update = wide_l[rs, :] * graft
            halves = [update[:, h * 2 * cw:(h + 1) * 2 * cw].reshape(rb // 8, 8, 2 * cw) for h in range(2)]
            upd[pl.ds(i * (rb // 8), rb // 8)] = jnp.concatenate(halves, axis=1).astype(BF16)

        def send_back(d):
            pltpu.make_async_remote_copy(
                src_ref=upd.at[d], dst_ref=rbuf.at[own_site],
                send_sem=u_send, recv_sem=u_recv,
                device_id=there(z, d), device_id_type=MESH).start()

        each_peer(0, hb, send_back)
        rbuf[own_site] = upd[me]
        settle(rbuf.at[pl.ds(0, grp - 1)], u_recv)
        settle(upd.at[pl.ds(0, nb - 1)], u_send)

    @pl.when(jnp.logical_not(is_site))
    def _():
        settle(rbuf, u_recv)

    returned = rbuf[...].astype(F32).reshape(grp, 2, 8, 2 * cw)
    for h in range(2):
        out[:, h * 2 * cw:(h + 1) * 2 * cw] = returned[:, h].reshape(rows, 2 * cw).astype(BF16)

    settle(statbuf.at[pl.ds(0, nb - 1)], s_send)

    @pl.when(is_site)
    def _():
        settle(selbuf.at[pl.ds(0, grp - 1)], f_send)
        settle(diags.at[pl.ds(0, grp - 1)], d_send)
        settle(zstage.at[pl.ds(0, grp - 1)], g_send)

    @pl.when(jnp.logical_not(is_site))
    def _():
        settle(selbuf, f_send)
        settle(diags.at[pl.ds(0, grp)], d_send)
        settle(zstage, g_send)

    for k in range(4):
        for way in range(2):
            first = half - arc(k, way)

            @pl.loop(first, half)
            def _(s):
                hop(zrecv.at[way, k, s], way, k, s).wait_send()


def body(grad_part, owner_table, left_stats, right_stats):
    nz, nb = lax.axis_size("dp"), lax.axis_size("block")
    grp = owner_table.shape[0]
    order = left_stats.shape[-1]
    cw, rows, half = order // 4, grp * 8, nz // 2
    vmem, dma = pltpu.VMEM, pltpu.SemaphoreType.DMA
    out = pl.pallas_call(
        functools.partial(kernel, nz, nb, grp),
        out_shape=jax.ShapeDtypeStruct((rows, order), BF16),
        in_specs=[pl.BlockSpec(memory_space=pltpu.SMEM), pl.BlockSpec(memory_space=pltpu.HBM),
                  pl.BlockSpec(memory_space=pltpu.HBM), pl.BlockSpec(memory_space=pltpu.HBM)],
        out_specs=pl.BlockSpec(memory_space=pltpu.VMEM),
        scratch_shapes=[vmem((nz * rows, order), BF16), dma,
            vmem((2, 4, half, rows // 4, order), BF16), vmem((grp, 16, 2 * cw), BF16), vmem((nb, 16, 2 * cw), BF16),
            vmem((order, order), BF16), vmem((order, order), BF16), vmem((2, order, 2 * cw), BF16),
            vmem((nb, 16, 2 * cw), BF16), vmem((grp, 16, 2 * cw), BF16), vmem((nb, 16, 2 * cw), BF16),
            vmem((order, order), BF16), vmem((order, order), BF16),
            vmem((8, cw), F32), vmem((nb, 8, cw), F32),
            vmem((order, order), BF16), vmem((order, order), BF16),
            vmem((order, order), F32), vmem((order, order), F32),
            vmem((order, order), BF16), vmem((order, order), BF16), vmem((order, order), BF16),
            vmem((order, order), BF16), vmem((order, order), BF16), vmem((order, order), BF16),
            vmem((nb, 16, 2 * cw), BF16), vmem((grp, 16, 2 * cw), BF16),
            dma((2, 4, half)), dma((2, 4, half)), dma, dma,
            dma, dma, dma, dma, dma, dma, dma, dma, dma, dma,
            pltpu.SemaphoreType.REGULAR((4,)),
        ],
        compiler_params=pltpu.CompilerParams(
            collective_id=0, has_side_effects=True, vmem_limit_bytes=53 * 1024 * 1024 + 512 * 1024),
    )(owner_table, grad_part.reshape(nz * rows, order), left_stats[0, 0], right_stats[0, 0])
    return out.reshape(grp, 8, order)


def solution(mesh):
    placed = (
        P("dp", None, "block", None),
        P("dp"),
        P("dp", "block", None, None),
        P("dp", "block", None, None),
    )
    return jax.shard_map(
        body, mesh=mesh, in_specs=placed, out_specs=P("dp", "block", None), check_vma=False
    )
```

```python
import functools

import jax
import jax.numpy as jnp
from jax import lax
from jax.experimental import pallas as pl
from jax.experimental.pallas import tpu as pltpu
from jax.sharding import PartitionSpec as P

DECAY = 0.9
EPSILON = 1e-06
MESH = pl.DeviceIdType.MESH
F32 = jnp.float32
BF16 = jnp.bfloat16


def zigzag(i, n):
    return n // 2 + jnp.where(lax.rem(i, 2) == 1, -((i + 1) // 2), i // 2)


def wide_dot(a, b, contract):
    return lax.dot_general(a, b, ((contract[0], contract[1]), ((), ())), preferred_element_type=F32)


def kernel(nz, nb, grp, table, gp_hbm, left, right, out, gp, gp_sem,
           zrecv, zstage, gbuf, l_ref, r_ref, pair, statbuf, selbuf, statfull, m_ref, mt_ref,
           diag, diags, g_ref, gt_ref,
           wide_l, wide_r, low_l, low_r, sq_l, sq_r, mix_l, mix_r, upd, rbuf,
           z_send, z_recv, g_send, g_recv, s_send, s_recv, f_send, f_recv, u_send, u_recv, d_send, d_recv,
           l_sem, r_sem, token):
    z = lax.axis_index("dp")
    me = lax.axis_index("block")
    order = 8 * nb
    cw = order // 4
    rows = grp * 8
    half = nz // 2
    few = grp // 4

    def site_of(j):
        place = 4 * lax.rem(j, few) + j // few
        return 4 * place + 2 * lax.rem(place // 2, 2) + 1

    def block_at(place):
        return lax.rem(place, 4) * few + place // 4

    own_site = block_at(me // 4)
    is_site = me == site_of(own_site)

    def there(dp, block):
        return {"dp": dp, "block": block}

    up, down = lax.rem(z + 1, nz), lax.rem(z + nz - 1, nz)
    hb = nb // 2
    load = pltpu.make_async_copy(gp_hbm, gp, gp_sem)
    load.start()
    load_l = pltpu.make_async_copy(left, l_ref, l_sem)
    load_l.start()
    load_r = pltpu.make_async_copy(right, r_ref, r_sem)
    load_r.start()

    def each_peer(low, high, act):
        if low == 0:
            act(lax.rem(me + hb, nb))
            low = 1

        @pl.loop(low, high)
        def _(i):
            act(lax.rem(me + (hb + i), nb))
            act(lax.rem(me + (hb - i), nb))

    def peer_site(i):
        return block_at(lax.rem(me // 4 + zigzag(i, grp), grp))

    cores, width = 2, 4
    height = nb // (cores * width)
    y, x, c = me // (cores * width), lax.rem(me // cores, width), lax.rem(me, cores)

    def moved(dy, dx, dc):
        return (lax.rem(y + dy + height, height) * width + lax.rem(x + dx + width, width)) * cores + lax.rem(c + dc, cores)

    late = z >= half
    barrier = pltpu.get_barrier_semaphore()

    def tell(semaphore, dp, block):
        pl.semaphore_signal(semaphore, inc=1, device_id=there(dp, block), device_id_type=MESH)

    for neighbour in (up, down):
        tell(barrier, neighbour, me)

    @pl.when(late)
    def _():
        for dy, dx, dc in ((1, 0, 0), (-1, 0, 0), (0, 1, 0), (0, -1, 0), (0, 0, 1)):
            tell(barrier, z, moved(dy, dx, dc))

    @pl.when(jnp.logical_not(late))
    def _():
        each_peer(0, hb, lambda d: tell(barrier, z, d))

    rounds = [((1, 0, 0), (-1, 0, 0), (0, 0, 1)),
              ((2, 0, 0), (-2, 0, 0)) if height > 4 else (),
              ((0, 1, 0), (0, -1, 0), (0, 1, 1), (0, -1, 1), (0, 0, 1)),
              ((0, 2, 0), (0, 2, 1))]

    def give(r):
        @pl.when(late)
        def _():
            for step in rounds[r]:
                tell(token.at[r], z, moved(*step))

    def take(r):
        @pl.when(late)
        def _():
            if rounds[r]:
                pl.semaphore_wait(token.at[r], len(rounds[r]))

    def spread(low, high):
        def act(d):
            pltpu.make_async_remote_copy(
                src_ref=pair.at[d // hb, pl.ds(pl.multiple_of(16 * lax.rem(d, hb), 16), 16)], dst_ref=statbuf.at[me],
                send_sem=s_send, recv_sem=s_recv, device_id=there(z, d), device_id_type=MESH).start()

        each_peer(low, high, act)

    def spread_diagonal():
        @pl.loop(0, grp)
        def _(i):
            who = site_of(peer_site(i))

            @pl.when(who != me)
            def _():
                pltpu.make_async_remote_copy(
                    src_ref=diag, dst_ref=diags.at[me], send_sem=d_send, recv_sem=d_recv,
                    device_id=there(z, who), device_id_type=MESH).start()

    part = rows // 4

    def own_part(d, k, held=gp):
        return held.at[pl.ds(pl.multiple_of(d * rows + k * part, part), part), :]

    def arc(k, way):
        return half if (k + way) % 2 == 0 else half - 1

    def hop(src, way, k, s):
        return pltpu.make_async_remote_copy(
            src_ref=src, dst_ref=zrecv.at[way, k, s],
            send_sem=z_send.at[way, k, s], recv_sem=z_recv.at[way, k, s],
            device_id=there(up if way == 0 else down, me), device_id_type=MESH)

    def target(way, dist):
        return lax.rem(z + dist, nz) if way == 0 else lax.rem(z + nz - dist, nz)

    def begin(s, ways):
        for k in range(4):
            for way in ways:
                if half - arc(k, way) == s:
                    d = target(way, half - s)
                    hop(own_part(d, k, gp_hbm), way, k, s).start()

    def onward(s, k, way):
        held = zrecv.at[way, k, s - 1]
        hop(held, way, k, s - 1).wait_recv()
        d = target(way, half - s)
        held[...] = (held[...].astype(F32) + own_part(d, k)[...].astype(F32)).astype(BF16)
        hop(held, way, k, s).start()

    def settle(ref, sem):
        pltpu.make_async_copy(ref, ref, sem).wait()

    def relay():
        settle(statbuf.at[pl.ds(0, nb - 1)], s_recv)

        @pl.loop(0, grp)
        def _(i):
            j = peer_site(i)
            selbuf[j] = statbuf[table[j]]
            who = site_of(j)

            @pl.when(who != me)
            def _():
                pltpu.make_async_remote_copy(
                    src_ref=selbuf.at[j], dst_ref=statfull.at[me],
                    send_sem=f_send, recv_sem=f_recv,
                    device_id=there(z, who), device_id_type=MESH).start()

        @pl.when(is_site)
        def _():
            statfull[me] = selbuf[own_site]

    third = hb // 3

    @pl.when(late)
    def _():
        pl.semaphore_wait(barrier, 7)

    @pl.when(jnp.logical_not(late))
    def _():
        pl.semaphore_wait(barrier, nb + 1)

    begin(0, (0, 1))
    begin(1, (0, 1))
    give(0)

    load_l.wait()
    load_r.wait()
    rb4 = order // 4
    for i in range(4):
        rs = pl.ds(i * rb4, rb4)
        row = lax.broadcasted_iota(jnp.int32, (rb4, order), 0) + i * rb4
        col = lax.broadcasted_iota(jnp.int32, (rb4, order), 1)
        right_rows = r_ref[rs, :].astype(F32)
        both = jnp.where(col >= row, l_ref[rs, :].astype(F32), right_rows).astype(BF16)
        for h in range(2):
            pair[h, rs, :] = both[:, h * 2 * cw:(h + 1) * 2 * cw]
        on_diagonal = jnp.sum(jnp.where(col == row, right_rows, 0.0), axis=0, keepdims=True)
        diag[pl.ds(i, 1), :] = on_diagonal[:, i * cw:(i + 1) * cw]
    diag[pl.ds(4, 4), :] = jnp.zeros((4, cw), F32)
    statbuf[me] = pair[me // hb, pl.ds(pl.multiple_of(16 * lax.rem(me, hb), 16), 16), :]

    @pl.when(is_site)
    def _():
        diags[me] = diag[...]

    @pl.when(jnp.logical_not(late))
    def _():
        spread(0, hb)
        spread_diagonal()

    load.wait()
    take(0)
    give(1)
    for k in range(4):
        for way in range(2):
            if arc(k, way) == half:
                onward(1, k, way)
    take(1)
    give(2)

    def some_onward(s, low, high):
        for k in range(low, high):
            for way in range(2):
                onward(s, k, way)

    if half > 2:
        some_onward(2, 0, 2)
    take(2)
    give(3)
    if half > 2:
        some_onward(2, 2, 4)
    take(3)

    @pl.when(late)
    def _():
        spread(0, 2 * third)

    if half > 3:
        some_onward(3, 0, 4)

    @pl.when(late)
    def _():
        spread(2 * third, hb)
        spread_diagonal()

    @pl.loop(4, half - 1)
    def _(s):
        some_onward(s, 0, 4)

    @pl.when(jnp.logical_not(late))
    def _():
        relay()

    if half > 4:
        some_onward(half - 1, 0, 4)

    for k in range(4):
        total = own_part(z, k)[...].astype(F32)
        for way in range(2):
            hop(zrecv.at[way, k, half - 1], way, k, half - 1).wait_recv()
            total = total + zrecv[way, k, half - 1].astype(F32)
        halves = [total[:, h * 2 * cw:(h + 1) * 2 * cw].reshape(few, 8, 2 * cw) for h in range(2)]
        zstage[pl.ds(k * few, few)] = jnp.concatenate(halves, axis=1).astype(BF16)

        @pl.loop(k * few, (k + 1) * few)
        def _(j):
            who = site_of(j)

            @pl.when(who != me)
            def _():
                pltpu.make_async_remote_copy(
                    src_ref=zstage.at[j], dst_ref=gbuf.at[me], send_sem=g_send, recv_sem=g_recv,
                    device_id=there(z, who), device_id_type=MESH).start()

            @pl.when(who == me)
            def _():
                gbuf[me] = zstage[j]

    @pl.when(late)
    def _():
        relay()

    @pl.when(is_site)
    def _():
        settle(diags.at[pl.ds(0, nb - 1)], d_recv)
        chosen = diags[table[own_site]]
        right_diag = jnp.concatenate([chosen[i:i + 1, :] for i in range(4)], axis=1)
        settle(statfull.at[pl.ds(0, nb - 1)], f_recv)
        for h in range(2):
            columns = statfull[pl.ds(h * hb, hb)].reshape(order, 2 * cw)
            m_ref[:, h * 2 * cw:(h + 1) * 2 * cw] = columns
            mt_ref[h * 2 * cw:(h + 1) * 2 * cw, :] = columns.T
        nr = 2
        rb = order // nr
        blocks = [pl.ds(i * rb, rb) for i in range(nr)]
        for i, rs in enumerate(blocks):
            row = lax.broadcasted_iota(jnp.int32, (rb, order), 0) + i * rb
            col = lax.broadcasted_iota(jnp.int32, (rb, order), 1)
            stored, turned = m_ref[rs, :].astype(F32), mt_ref[rs, :].astype(F32)
            wide_l[rs, :] = DECAY * jnp.where(col >= row, stored, turned)
            wide_r[rs, :] = DECAY * jnp.where(col == row, right_diag, jnp.where(col > row, turned, stored))
        settle(gbuf.at[pl.ds(0, nb - 1)], g_recv)
        pieces = gbuf[...].astype(F32).reshape(nb, 2, 8, 2 * cw)
        for h in range(2):
            piece = pieces[:, h].reshape(order, 2 * cw).astype(BF16)
            g_ref[:, h * 2 * cw:(h + 1) * 2 * cw] = piece
            gt_ref[h * 2 * cw:(h + 1) * 2 * cw, :] = piece.T
        sides = ((0, g_ref, gt_ref, wide_l, low_l, sq_l, mix_l), (1, gt_ref, g_ref, wide_r, low_r, sq_r, mix_r))
        bounds = []
        for side, a, b, wide, low, sq, mix in sides:
            sums = jnp.zeros((1, order), F32)
            for i, rs in enumerate(blocks):
                stat = wide[rs, :] + (1.0 - DECAY) * wide_dot(a[rs, :], b[...], ((1,), (0,)))
                wide[rs, :] = stat
                sums = sums + jnp.sum(jnp.abs(stat), axis=0, keepdims=True)
            bounds.append(jnp.max(sums, axis=1, keepdims=True))
        for (side, a, b, wide, low, sq, mix), bound in zip(sides, bounds):
            scale = 1.0 / bound
            for rs in blocks:
                scaled = wide[rs, :] * scale
                wide[rs, :] = scaled
                low[rs, :] = scaled.astype(BF16)
        for side, a, b, wide, low, sq, mix in sides:
            for rs in blocks:
                square = wide_dot(low[rs, :], low[...], ((1,), (0,))).astype(BF16)
                sq[rs, :] = square
                mix[rs, :] = (square.astype(F32) - 9.0 * wide[rs, :]).astype(BF16)
        for side, a, b, wide, low, sq, mix in sides:
            for i, rs in enumerate(blocks):
                eye = (lax.broadcasted_iota(jnp.int32, (rb, order), 0) + i * rb
                       == lax.broadcasted_iota(jnp.int32, (rb, order), 1)).astype(F32)
                square = sq[rs, :]
                quartic = wide_dot(square, mix[...], ((1,), (0,)))
                low[rs, :] = (36.0 * eye - 39.0 * wide[rs, :] + 27.0 * square.astype(F32) + quartic).astype(BF16)
        grad_sum = jnp.zeros((1, order), F32)
        cond_sum = jnp.zeros((1, order), F32)
        for rs in blocks:
            done = wide_dot(low_l[rs, :], g_ref[...], ((1,), (0,))).astype(BF16)
            cond = wide_dot(done, low_r[...], ((1,), (0,)))
            wide_l[rs, :] = cond
            grad = g_ref[rs, :].astype(F32)
            grad_sum = grad_sum + jnp.sum(grad * grad, axis=0, keepdims=True)
            cond_sum = cond_sum + jnp.sum(cond * cond, axis=0, keepdims=True)
        count = 1.0 / (order * order)
        grad_power = jnp.sum(grad_sum, axis=1, keepdims=True) * count
        cond_power = jnp.sum(cond_sum, axis=1, keepdims=True) * count
        graft = jnp.sqrt(grad_power) / jnp.sqrt(cond_power + EPSILON)
        for i, rs in enumerate(blocks):
            update = wide_l[rs, :] * graft
            halves = [update[:, h * 2 * cw:(h + 1) * 2 * cw].reshape(rb // 8, 8, 2 * cw) for h in range(2)]
            upd[pl.ds(i * (rb // 8), rb // 8)] = jnp.concatenate(halves, axis=1).astype(BF16)

        def send_back(d):
            pltpu.make_async_remote_copy(
                src_ref=upd.at[d], dst_ref=rbuf.at[own_site],
                send_sem=u_send, recv_sem=u_recv,
                device_id=there(z, d), device_id_type=MESH).start()

        each_peer(0, hb, send_back)
        rbuf[own_site] = upd[me]
        settle(rbuf.at[pl.ds(0, grp - 1)], u_recv)
        settle(upd.at[pl.ds(0, nb - 1)], u_send)

    @pl.when(jnp.logical_not(is_site))
    def _():
        settle(rbuf, u_recv)

    returned = rbuf[...].astype(F32).reshape(grp, 2, 8, 2 * cw)
    for h in range(2):
        out[:, h * 2 * cw:(h + 1) * 2 * cw] = returned[:, h].reshape(rows, 2 * cw).astype(BF16)

    settle(statbuf.at[pl.ds(0, nb - 1)], s_send)

    @pl.when(is_site)
    def _():
        settle(selbuf.at[pl.ds(0, grp - 1)], f_send)
        settle(diags.at[pl.ds(0, grp - 1)], d_send)
        settle(zstage.at[pl.ds(0, grp - 1)], g_send)

    @pl.when(jnp.logical_not(is_site))
    def _():
        settle(selbuf, f_send)
        settle(diags.at[pl.ds(0, grp)], d_send)
        settle(zstage, g_send)

    for k in range(4):
        for way in range(2):
            first = half - arc(k, way)

            @pl.loop(first, half)
            def _(s):
                hop(zrecv.at[way, k, s], way, k, s).wait_send()


def body(grad_part, owner_table, left_stats, right_stats):
    nz, nb = lax.axis_size("dp"), lax.axis_size("block")
    grp = owner_table.shape[0]
    order = left_stats.shape[-1]
    cw, rows, half = order // 4, grp * 8, nz // 2
    vmem, dma = pltpu.VMEM, pltpu.SemaphoreType.DMA
    out = pl.pallas_call(
        functools.partial(kernel, nz, nb, grp),
        out_shape=jax.ShapeDtypeStruct((rows, order), BF16),
        in_specs=[pl.BlockSpec(memory_space=pltpu.SMEM), pl.BlockSpec(memory_space=pltpu.HBM),
                  pl.BlockSpec(memory_space=pltpu.HBM), pl.BlockSpec(memory_space=pltpu.HBM)],
        out_specs=pl.BlockSpec(memory_space=pltpu.VMEM),
        scratch_shapes=[vmem((nz * rows, order), BF16), dma,
            vmem((2, 4, half, rows // 4, order), BF16), vmem((grp, 16, 2 * cw), BF16), vmem((nb, 16, 2 * cw), BF16),
            vmem((order, order), BF16), vmem((order, order), BF16), vmem((2, order, 2 * cw), BF16),
            vmem((nb, 16, 2 * cw), BF16), vmem((grp, 16, 2 * cw), BF16), vmem((nb, 16, 2 * cw), BF16),
            vmem((order, order), BF16), vmem((order, order), BF16),
            vmem((8, cw), F32), vmem((nb, 8, cw), F32),
            vmem((order, order), BF16), vmem((order, order), BF16),
            vmem((order, order), F32), vmem((order, order), F32),
            vmem((order, order), BF16), vmem((order, order), BF16), vmem((order, order), BF16),
            vmem((order, order), BF16), vmem((order, order), BF16), vmem((order, order), BF16),
            vmem((nb, 16, 2 * cw), BF16), vmem((grp, 16, 2 * cw), BF16),
            dma((2, 4, half)), dma((2, 4, half)), dma, dma,
            dma, dma, dma, dma, dma, dma, dma, dma, dma, dma,
            pltpu.SemaphoreType.REGULAR((4,)),
        ],
        compiler_params=pltpu.CompilerParams(
            collective_id=0, has_side_effects=True, vmem_limit_bytes=53 * 1024 * 1024 + 512 * 1024),
    )(owner_table, grad_part.reshape(nz * rows, order), left_stats[0, 0], right_stats[0, 0])
    return out.reshape(grp, 8, order)


def solution(mesh):
    placed = (
        P("dp", None, "block", None),
        P("dp"),
        P("dp", "block", None, None),
        P("dp", "block", None, None),
    )
    return jax.shard_map(
        body, mesh=mesh, in_specs=placed, out_specs=P("dp", "block", None), check_vma=False
    )
```
